32 devices in a mesh: job: 2 (over x), unit: 16 (over z, y, core).
Axes of the slice: x: 2, y: 2, z: 4, core: 2. Of those that a mesh axis runs over, the one named last changes fastest.
Arguments:
- query_grad: bfloat16 [16384, 28672], P('job', 'unit'), parts along dimension 0, may hold values from -0.00036621094 to 0.00036621094
- out_grads: bfloat16 [512, 8192], P(('job', 'unit')), parts along dimension 0, may hold values from -6 to 6
- inputs: bfloat16 [512, 28672], P('job', 'unit'), parts along dimension 0, may hold values from -6 to 6
Outputs:
- scores: float32 [512], P('job'), parts along dimension 0
The draws below stay inside these ranges and needn't reach their ends.
There are 2 independent parts, one for each index of `job`. The reference program is written for one: setup_inputs(seed, part) draws one part's arguments, and reference() takes and returns one part's arrays. A program takes and returns all parts, laid end to end along the dimension named above; each array names one. Nothing has to cross between parts.
All inputs are finite; a program needn't handle non-finite values.
Results may differ from the reference program's by a relative error of at most 0.0003.
Values may be sent and summed in bfloat16 or wider, within the bound.
No kernel may reach another device: no remote copies, remote signals or barrier semaphores. Data moves between devices by JAX's collectives and lax.ppermute only.
A program may use at most 128 MiB of HBM per device.

```python
import jax
import jax.numpy as jnp
from jax import lax

D = 8192
FF = 28672
TOKENS = 256
BLOCK = 128


def level_of(key, dims, shards, least, top_value):
    factor_of, own = 1.0, jax.random.fold_in(key, 6)
    for dim, parts in shards:
        heights = jnp.exp(jax.random.uniform(jax.random.fold_in(own, dim), (parts,), jnp.float32, least / len(shards), top_value / len(shards)))
        factor_of = factor_of * jnp.repeat(heights, dims[dim] // parts).reshape([-1 if axis == dim else 1 for axis in range(len(dims))])
    return factor_of


def noise(key, dims, scale, bound, pieces=(), dtype=jnp.bfloat16):
    drawn = scale * jax.random.normal(key, dims, jnp.float32)
    if pieces:
        drawn = drawn * level_of(key, dims, pieces, -0.22, 0.18)
    return jnp.clip(drawn, -bound, bound).astype(dtype)


def setup_inputs(seed: int = 0, part: int = 0) -> dict:
    key_of = jax.random.split(jax.random.key(seed), 4)
    part_splits = jax.random.split(jax.random.fold_in(key_of[3], part), 4)
    query_grad = noise(part_splits[0], (D, FF), (D * FF) ** -0.5, 0.00036621094, ((1, 16),))
    out_grads = noise(part_splits[1], (TOKENS, D), 1.0, 6.0, ((0, 16),))
    inputs = noise(part_splits[2], (TOKENS, FF), 1.0, 6.0, ((1, 16),))
    return dict(query_grad=query_grad, out_grads=out_grads, inputs=inputs)


def reference(query_grad, out_grads, inputs):
    token_count = out_grads.shape[0]
    grouped_grads = out_grads.reshape(token_count // BLOCK, BLOCK, out_grads.shape[1])
    grouped_inputs = inputs.reshape(token_count // BLOCK, BLOCK, inputs.shape[1])

    def score_block(blocks):
        grads, values = blocks
        projected = jnp.dot(grads, query_grad, preferred_element_type=jnp.float32)
        return jnp.sum(projected * values.astype(jnp.float32), axis=1)

    return lax.map(score_block, (grouped_grads, grouped_inputs)).reshape(token_count)
```

```python
import functools

import jax
import jax.numpy as jnp
import numpy as np
from jax import lax
from jax.experimental import pallas as pl
from jax.experimental.pallas import tpu as pltpu
from jax.sharding import PartitionSpec as P

PIECES = 4
STEP = 1024
LANES = 128
VMEM = pl.BlockSpec(memory_space=pltpu.VMEM)


def ring_of(units):
    chips = units // 2
    if units != 16:
        return [2 * chip for chip in range(chips)]
    there = [2 * chip for chip in range(0, chips, 2)]
    return there + [2 * chip for chip in range(chips - 1, 0, -2)]


def plan(units):
    ring = ring_of(units)
    chips = len(ring)
    at = lambda place, core: ring[place % chips] + core
    ahead, across, twin = [], [], []
    held = np.zeros((units, chips), np.int32)
    for place in range(chips):
        for core, way in ((0, 1), (1, -1)):
            me = at(place, core)
            ahead.append((me, at(place + way, core)))
            across.append((at(place, 1 - core), at(place + way, core)))
            twin.append((me, at(place, 1 - core)))
            blocks = [me]
            for hop in range(1, chips // 2):
                blocks += [at(place - way * hop, core), at(place - way * hop, 1 - core)]
            blocks.append(at(place - way * (chips // 2), core))
            held[me] = blocks
    other = np.array([dict(twin)[unit] for unit in range(units)])
    return ahead, across, twin, np.concatenate([held, held[other]], axis=1)


def weigh_kernel(first, order, x_ref, q_ref, keep_ref, send_ref, rows):
    block = x_ref.shape[0] // order.shape[0]
    for place in range(order.shape[0]):
        start = pl.multiple_of(order[place] * block, block)
        rows[place * block : (place + 1) * block, :] = x_ref[pl.ds(start, block), :]
    half = keep_ref.shape[0]
    step = min(STEP, keep_ref.shape[1])

    @pl.loop(0, keep_ref.shape[1] // step)
    def _(i):
        at = pl.multiple_of(i * step, step)
        value = lax.dot_general(
            rows[...],
            q_ref[pl.ds(first + at, step), :],
            (((1,), (1,)), ((), ())),
            preferred_element_type=jnp.float32,
        )
        keep_ref[:, pl.ds(at, step)] = value[:half]
        send_ref[:, pl.ds(at, step)] = value[half:]


def weigh(first, width, order, x, q):
    tokens, depth = x.shape
    half = jax.ShapeDtypeStruct((tokens // 2, width), jnp.float32)
    return pl.pallas_call(
        functools.partial(weigh_kernel, first),
        in_specs=[pl.BlockSpec(memory_space=pltpu.SMEM), VMEM, VMEM],
        out_specs=[VMEM, VMEM],
        out_shape=[pltpu.VMEM(half.shape, half.dtype), half],
        scratch_shapes=[pltpu.VMEM((tokens, depth), x.dtype)],
        compiler_params=pltpu.CompilerParams(vmem_limit_bytes=12 << 20),
        cost_estimate=pl.CostEstimate(
            flops=2 * tokens * depth * width,
            bytes_accessed=2 * depth * width,
            transcendentals=0,
        ),
    )(order, x, q)


def dots(gradient, row, mine, theirs):
    block = gradient.shape[0]
    total = jnp.zeros((block, LANES), jnp.float32)
    width = mine[0].shape[1]
    for piece in range(len(mine)):
        for lane in range(0, width, LANES):
            weight = (
                mine[piece][row : row + block, lane : lane + LANES]
                + theirs[piece][row : row + block, lane : lane + LANES]
            )
            at = piece * width + lane
            total += gradient[:, at : at + LANES].astype(jnp.float32) * weight
    return total


def early_kernel(count, *refs):
    gradients, mine, theirs = refs[:count], refs[count : count + PIECES], refs[count + PIECES : -1]
    block = gradients[0].shape[0]
    for index in range(count):
        refs[-1][index * block : (index + 1) * block, :] = dots(
            gradients[index], index * block, mine, theirs
        )


def last_kernel(order, gradient, *refs):
    early, out, table = refs[-3:]
    mine, theirs = refs[:PIECES], refs[PIECES : 2 * PIECES]
    block = gradient.shape[0]
    blocks = early.shape[0] // block
    table[...] = jnp.zeros_like(table)
    for place in range(blocks):
        start = pl.multiple_of(order[place] * block, block)
        table[pl.ds(start, block), :] = early[place * block : (place + 1) * block, :]
    start = pl.multiple_of(order[blocks] * block, block)
    table[pl.ds(start, block), :] = dots(gradient, blocks * block, mine, theirs)
    out[...] = jnp.sum(table[...].T, axis=0, keepdims=True)


def in_vmem(arrays):
    return [pltpu.with_memory_space_constraint(array, pltpu.VMEM) for array in arrays]


def body(units, query_grad, out_grads, inputs):
    ahead, across, twin, orders = plan(units)
    send = lambda value, pairs: lax.ppermute(value, "unit", pairs)
    order = jnp.asarray(orders)[lax.axis_index("unit")]
    tokens = inputs.shape[0]
    block = out_grads.shape[0]
    width = query_grad.shape[0] // PIECES

    held = [out_grads, send(out_grads, ahead), send(out_grads, across)]
    for hop in range(2, units // 4):
        held += [send(held[-2], ahead), send(held[-1], ahead)]
    last = send(held[-2], ahead)

    q = pltpu.with_memory_space_constraint(query_grad, pltpu.VMEM)
    mine, theirs = [], []
    for piece in range(PIECES):
        keep, give = weigh(piece * width, width, order, inputs, q)
        mine.append(keep)
        theirs.append(send(give, twin))

    early = pl.pallas_call(
        functools.partial(early_kernel, len(held)),
        in_specs=[VMEM] * (len(held) + 2 * PIECES),
        out_specs=VMEM,
        out_shape=jax.ShapeDtypeStruct((len(held) * block, LANES), jnp.float32),
        compiler_params=pltpu.CompilerParams(vmem_limit_bytes=12 << 20),
    )(*held, *in_vmem(mine), *in_vmem(theirs))
    partial_value = pl.pallas_call(
        last_kernel,
        in_specs=[pl.BlockSpec(memory_space=pltpu.SMEM)] + [VMEM] * (2 + 2 * PIECES),
        out_specs=VMEM,
        out_shape=jax.ShapeDtypeStruct((1, tokens), jnp.float32),
        scratch_shapes=[pltpu.VMEM((tokens, LANES), jnp.float32)],
        compiler_params=pltpu.CompilerParams(vmem_limit_bytes=12 << 20),
    )(order, last, *in_vmem(mine), *in_vmem(theirs), early)

    bit = 1
    while bit < units:
        pairs = [(unit, unit ^ bit) for unit in range(units)]
        partial_value += send(partial_value, pairs)
        bit *= 2
    return partial_value.reshape(tokens)


def solution(mesh):
    return jax.shard_map(
        functools.partial(body, mesh.shape["unit"]),
        mesh=mesh,
        in_specs=(P("job", "unit"), P(("job", "unit"), None), P("job", "unit")),
        out_specs=P("job"),
        check_vma=False,
    )
```

```python
import functools

import jax
import jax.numpy as jnp
import numpy as np
from jax import lax
from jax.experimental import pallas as pl
from jax.experimental.pallas import tpu as pltpu
from jax.sharding import PartitionSpec as P

SPLIT = (2048, 2048, 2048, 2048)
STEP = 512
LANES = 128
SLOTS = 3
GROUP = 14
GRANT = 10 << 20
VMEM = pl.BlockSpec(memory_space=pltpu.VMEM)
SMEM = pl.BlockSpec(memory_space=pltpu.SMEM)
HBM = pl.BlockSpec(memory_space=pltpu.HBM)
ANY = pl.BlockSpec(memory_space=pl.ANY)


def ring_of(units):
    chips = units // 2
    if units != 16:
        return [2 * chip for chip in range(chips)]
    there = [2 * chip for chip in range(0, chips, 2)]
    return there + [2 * chip for chip in range(chips - 1, 0, -2)]


def plan(units):
    ring = ring_of(units)
    chips = len(ring)
    at = lambda place, core: ring[place % chips] + core
    ahead, across, twin = [], [], []
    held = np.zeros((units, chips), np.int32)
    for place in range(chips):
        for core, way in ((0, 1), (1, -1)):
            me = at(place, core)
            ahead.append((me, at(place + way, core)))
            across.append((at(place, 1 - core), at(place + way, core)))
            twin.append((me, at(place, 1 - core)))
            blocks = [me]
            for hop in range(1, chips // 2):
                blocks += [at(place - way * hop, core), at(place - way * hop, 1 - core)]
            blocks.append(at(place - way * (chips // 2), core))
            held[me] = blocks
    other = np.array([dict(twin)[unit] for unit in range(units)])
    return ahead, across, twin, np.concatenate([held, held[other]], axis=1)


def weigh_kernel(first, width, following, waits, order, x_ref, q_ref, *refs):
    steps = width // STEP
    begin = first == 0
    refs = list(refs)
    slab = None if begin else refs.pop(0)
    del refs[:waits]
    weights_ref = refs[1 if begin else 0]
    next_slab = refs[2 if begin else 1] if following else None

    def at(i):
        return pl.ds(pl.multiple_of(i * STEP, STEP), STEP)

    def fetch(start, i, to, sem, slots):
        here = pl.ds(pl.multiple_of(start + i * STEP, STEP), STEP)
        slot = lax.rem(i, slots)
        return pltpu.make_async_copy(q_ref.at[here], to.at[at(slot)], sem.at[slot])

    if begin:
        x, own, placed, ready, coming = refs[0], *refs[-4:]
        copy = pltpu.make_async_copy(x_ref, x, placed)
        copy.start()
        for i in range(SLOTS):
            fetch(first, i, own, ready, SLOTS).start()
        copy.wait()
    else:
        x, own, coming = x_ref, slab, refs[-1]
        for i in range(following // STEP):
            fetch(first + width, i, next_slab, coming, steps).start()

    @pl.loop(0, steps)
    def _(i):
        if begin:
            fetch(first, i, own, ready, SLOTS).wait()
        weights_ref[:, at(i)] = lax.dot_general(
            x[...],
            own[at(lax.rem(i, SLOTS) if begin else i), :],
            (((1,), (1,)), ((), ())),
            preferred_element_type=jnp.float32,
        )
        if begin:

            @pl.when(i + SLOTS < steps)
            def _():
                fetch(first, i + SLOTS, own, ready, SLOTS).start()

            @pl.when(i < following // STEP)
            def _():
                fetch(first + width, i, next_slab, coming, steps).start()

    for i in range(following // STEP):
        fetch(first + width, i, next_slab, coming, steps).wait()


def weigh(first, width, following, order, x, q, slab, after):
    tokens, depth = x.shape
    begin = first == 0
    out_shape, scratch = [], []
    if begin:
        out_shape.append(pltpu.VMEM(x.shape, x.dtype))
        scratch = [
            pltpu.VMEM((SLOTS * STEP, depth), q.dtype),
            pltpu.SemaphoreType.DMA,
            pltpu.SemaphoreType.DMA((SLOTS,)),
        ]
    out_shape.append(pltpu.VMEM((tokens, width), jnp.float32))
    if following:
        out_shape.append(pltpu.VMEM((following, depth), q.dtype))
    return pl.pallas_call(
        functools.partial(weigh_kernel, first, width, following, len(after)),
        in_specs=[SMEM] + ([HBM, HBM] if begin else [VMEM, HBM, VMEM] + [ANY] * len(after)),
        out_specs=[VMEM] * len(out_shape),
        out_shape=out_shape,
        scratch_shapes=scratch + [pltpu.SemaphoreType.DMA((max(following, STEP) // STEP,))],
        compiler_params=pltpu.CompilerParams(vmem_limit_bytes=GRANT),
        cost_estimate=pl.CostEstimate(
            flops=2 * tokens * depth * width,
            bytes_accessed=2 * depth * width,
            transcendentals=0,
        ),
    )(order, x, q, *([] if begin else [slab, *after]))


def dots(gradient, start, weights):
    block = gradient.shape[0]
    total = jnp.zeros((block, LANES), jnp.float32)
    at = 0
    for piece in weights:
        for lane in range(0, piece.shape[1], LANES):
            weight = piece[pl.ds(start, block), lane : lane + LANES]
            total += gradient[:, at : at + LANES].astype(jnp.float32) * weight
            at += LANES
    return total


def table_kernel(places, finish, order, *refs):
    count = len(places)
    gradients, weights = refs[:count], refs[count : count + len(SPLIT)]
    more = refs[count + len(SPLIT) :]
    out = more[-1]
    table = more[-1]
    if finish:
        out, table = more[-2:]
    if len(more) > 1 + finish:
        table[...] = more[0][...]
    else:
        table[...] = jnp.zeros_like(table)
    block = gradients[0].shape[0]
    for place, gradient in zip(places, gradients):
        start = pl.multiple_of(order[place] * block, block)
        table[pl.ds(start, block), :] = dots(gradient, start, weights)
    if finish:
        out[...] = jnp.sum(table[...].T, axis=0, keepdims=True)


def add_blocks(places, order, gradients, weights, table, finish):
    tokens = weights[0].shape[0]
    shape = (tokens, LANES)
    extra = [] if table is None else [table]
    return pl.pallas_call(
        functools.partial(table_kernel, places, finish),
        in_specs=[SMEM] + [VMEM] * (len(gradients) + len(weights) + len(extra)),
        out_specs=VMEM,
        out_shape=jax.ShapeDtypeStruct((1, tokens) if finish else shape, jnp.float32),
        scratch_shapes=[pltpu.VMEM(shape, jnp.float32)] * finish,
        compiler_params=pltpu.CompilerParams(vmem_limit_bytes=GRANT),
    )(order, *gradients, *weights, *extra)


def in_vmem(arrays):
    return [pltpu.with_memory_space_constraint(array, pltpu.VMEM) for array in arrays]


def body(units, query_grad, out_grads, inputs):
    ahead, across, twin, orders = plan(units)
    send = lambda value, pairs: lax.ppermute(value, "unit", pairs)
    order = jnp.asarray(orders)[lax.axis_index("unit")]
    tokens = inputs.shape[0]
    half = units // 2

    weights, slabs, rows = [], [], []
    resident = pltpu.with_memory_space_constraint(query_grad, pltpu.HBM)

    def piece(*after):
        done = len(weights)
        following = SPLIT[done + 1] if done + 1 < len(SPLIT) else 0
        x = rows[0] if done else pltpu.with_memory_space_constraint(inputs, pltpu.HBM)
        made = list(weigh(
            sum(SPLIT[:done]), SPLIT[done], following, order, x, resident, slabs[-1] if done else None, after
        ))
        if not done:
            rows.extend(in_vmem([made.pop(0)]))
        weights.extend(in_vmem([made.pop(0)]))
        slabs.extend(in_vmem(made))

    def later(value):
        return lax.optimization_barrier((value, weights[-1]))[0]

    hops = units // 4
    held = [out_grads, send(out_grads, ahead), send(out_grads, across)]
    piece()
    for hop in range(1, hops):
        same, other = held[-2:]
        held.append(send(later(same), ahead))
        if hop + 1 == hops:
            break
        if hop > 1 and len(weights) < len(SPLIT):
            piece(same)
        held.append(send(later(other) if hop > 1 else other, ahead))
        if len(weights) < len(SPLIT):
            piece(*([same, other] if hop == 1 else [other]))
    blocks = held + [send(value, twin) for value in held]

    final = [half - 1, units - 1]
    rest = [place for place in range(units) if place not in final]
    table = None
    for group in range(0, len(rest), GROUP):
        places = rest[group : group + GROUP]
        table = add_blocks(places, order, [blocks[place] for place in places], weights, table, False)
    partial_value = add_blocks(final, order, [blocks[place] for place in final], weights, table, True)

    bit = 1
    while bit < units:
        pairs = [(unit, unit ^ bit) for unit in range(units)]
        partial_value += send(partial_value, pairs)
        bit *= 2
    return partial_value.reshape(tokens)


def solution(mesh):
    return jax.shard_map(
        functools.partial(body, mesh.shape["unit"]),
        mesh=mesh,
        in_specs=(P("job", "unit"), P(("job", "unit"), None), P("job", "unit")),
        out_specs=P("job"),
        check_vma=False,
    )
```

```python
import functools

import jax
import jax.numpy as jnp
from jax import lax
from jax.experimental import pallas as pl
from jax.experimental.pallas import tpu as pltpu
from jax.sharding import PartitionSpec as P

SPLIT = (1024, 3072, 2048, 2048)
FETCH = 512
STEP = 1024
LANES = 128
GROUP = 16
TABLE_FLOPS = 2 * 10**10
GRANT = 8 << 20
VMEM = pl.BlockSpec(memory_space=pltpu.VMEM)
HBM = pl.BlockSpec(memory_space=pltpu.HBM)
ANY = pl.BlockSpec(memory_space=pl.ANY)


def place_of(units, unit):
    chips = units // 2
    chip = unit // 2
    if units != 16:
        return chip
    odd = chip % 2
    return (1 - odd) * (chip // 2) + odd * (chips - 1 - chip // 2)


def unit_at(units, place, core):
    chips = units // 2
    place = lax.rem(place + 2 * chips, chips)
    if units != 16:
        return 2 * place + core
    back = place // (chips // 2)
    return 2 * ((1 - back) * 2 * place + back * (2 * (chips - 1 - place) + 1)) + core


def block_of(units, hop, same, mine):
    unit = lax.axis_index("unit")
    core = lax.rem(unit, 2)
    holder = core if mine else 1 - core
    place = place_of(units, unit) - (1 - 2 * holder) * hop
    return unit_at(units, place, holder if same else 1 - holder)


def pairs_of(units):
    chips = units // 2
    walk = sorted(range(chips), key=lambda chip: place_of(units, 2 * chip))
    at = lambda place, core: 2 * walk[place % chips] + core
    ahead, across, twin = [], [], []
    for place in range(chips):
        for core, way in ((0, 1), (1, -1)):
            ahead.append((at(place, core), at(place + way, core)))
            across.append((at(place, 1 - core), at(place + way, core)))
            twin.append((at(place, core), at(place, 1 - core)))
    return ahead, across, twin


def product(rows, columns):
    return lax.dot_general(rows, columns, (((1,), (1,)), ((), ())), preferred_element_type=jnp.float32)


def fetches(q_ref, first, count, to, sems):
    return [
        pltpu.make_async_copy(
            q_ref.at[pl.ds(first + at, FETCH)], to.at[pl.ds(at, FETCH)], sems.at[at // FETCH]
        )
        for at in range(0, count, FETCH)
    ]


def first_kernel(width, following, x_ref, q_ref, x, weights, slab, own, placed, ready, coming):
    move = pltpu.make_async_copy(x_ref, x, placed)
    move.start()
    mine = fetches(q_ref, 0, width, own, ready)
    later = fetches(q_ref, width, following, slab, coming)
    for copy in mine + later:
        copy.start()
    move.wait()
    for index, copy in enumerate(mine):
        copy.wait()
        at = slice(index * FETCH, (index + 1) * FETCH)
        weights[:, at] = product(x[...], own[at, :])
    for copy in later:
        copy.wait()


def next_kernel(first, width, following, waits, x, q_ref, slab, *refs):
    weights = refs[waits]
    later = []
    if following:
        later = fetches(q_ref, first + width, following, refs[waits + 1], refs[-1])
    for copy in later:
        copy.start()

    @pl.loop(0, width // STEP)
    def _(i):
        at = pl.ds(pl.multiple_of(i * STEP, STEP), STEP)
        weights[:, at] = product(x[...], slab[at, :])

    for copy in later:
        copy.wait()


def weigh(piece, x, q, slab, after):
    tokens, depth = x.shape
    first, width = sum(SPLIT[:piece]), SPLIT[piece]
    following = SPLIT[piece + 1] if piece + 1 < len(SPLIT) else 0
    out_shape = [pltpu.VMEM((tokens, width), jnp.float32)]
    scratch = []
    if following:
        out_shape.append(pltpu.VMEM((following, depth), q.dtype))
        scratch = [pltpu.SemaphoreType.DMA((following // FETCH,))]
    if piece:
        kernel = functools.partial(next_kernel, first, width, following, len(after))
        operands = [x, q, slab, *after]
        in_specs = [VMEM, HBM, VMEM] + [ANY] * len(after)
    else:
        kernel = functools.partial(first_kernel, width, following)
        operands = [x, q]
        in_specs = [HBM, HBM]
        out_shape.insert(0, pltpu.VMEM(x.shape, x.dtype))
        scratch = [
            pltpu.VMEM((width, depth), q.dtype),
            pltpu.SemaphoreType.DMA,
            pltpu.SemaphoreType.DMA((width // FETCH,)),
        ] + scratch
    return pl.pallas_call(
        kernel,
        in_specs=in_specs,
        out_specs=[VMEM] * len(out_shape),
        out_shape=out_shape,
        scratch_shapes=scratch,
        compiler_params=pltpu.CompilerParams(vmem_limit_bytes=GRANT),
        cost_estimate=pl.CostEstimate(
            flops=2 * tokens * depth * width,
            bytes_accessed=2 * depth * width,
            transcendentals=0,
        ),
    )(*operands)


def dots(gradient, weights):
    total = jnp.zeros((gradient.shape[0], LANES), jnp.float32)
    at = 0
    for width, weight in zip(SPLIT, weights):
        for lane in range(0, width, LANES):
            total += gradient[:, at : at + LANES].astype(jnp.float32) * weight(lane)
            at += LANES
    return total


def rows_of(ref, start, block):
    return lambda lane: ref[pl.ds(start, block), lane : lane + LANES]


def stack_kernel(*refs):
    out, at = refs[-1], 0
    for ref in refs[:-1]:
        out[at : at + ref.shape[0], :] = ref[...]
        at += ref.shape[0]


def stack(arrays):
    rows = sum(array.shape[0] for array in arrays)
    return pl.pallas_call(
        stack_kernel,
        in_specs=[VMEM] * len(arrays),
        out_specs=VMEM,
        out_shape=jax.ShapeDtypeStruct((rows, arrays[0].shape[1]), arrays[0].dtype),
        compiler_params=pltpu.CompilerParams(vmem_limit_bytes=GRANT),
    )(*arrays)


def table_kernel(units, block, places, fresh, *refs):
    count = 1 + max(array for array, _, _ in places)
    gradients, weights, table = refs[:count], refs[count : count + len(SPLIT)], refs[-1]
    table[...] = jnp.zeros_like(table) if fresh else refs[-2][...]
    for array, row, place in places:
        start = pl.multiple_of(block_of(units, *place) * block, block)
        gradient = gradients[array][row : row + block, :]
        table[pl.ds(start, block), :] = dots(gradient, [rows_of(ref, start, block) for ref in weights])


def add_blocks(units, block, found, weights, table, flops):
    shape = (weights[0].shape[0], LANES)
    arrays, places = [], []
    for place, array, row in found:
        if not any(array is known for known in arrays):
            arrays.append(array)
        index = [array is known for known in arrays].index(True)
        places.append((index, row, place))
    extra = [] if table is None else [table]
    return pl.pallas_call(
        functools.partial(table_kernel, units, block, places, table is None),
        in_specs=[VMEM] * (len(arrays) + len(weights) + len(extra)),
        out_specs=VMEM,
        out_shape=jax.ShapeDtypeStruct(shape, jnp.float32),
        compiler_params=pltpu.CompilerParams(vmem_limit_bytes=GRANT),
        cost_estimate=pl.CostEstimate(flops=flops, bytes_accessed=0, transcendentals=0),
    )(*arrays, *weights, *extra)


def give_kernel(units, places, *refs):
    weights, out = refs[:-1], refs[-1]
    block = out.shape[0] // len(places)
    for index, place in enumerate(places):
        start = pl.multiple_of(block_of(units, *place, False) * block, block)
        at = 0
        for ref in weights:
            out[index * block : (index + 1) * block, at : at + ref.shape[1]] = ref[pl.ds(start, block), :]
            at += ref.shape[1]


def last_kernel(units, block, places, *refs):
    gradients, refs = refs[: len(places)], refs[len(places) :]
    theirs, table, *weights, out, full = refs
    full[...] = table[...]

    def rows(place):
        return pl.ds(pl.multiple_of(block_of(units, *place) * block, block), block)

    for index, (gradient, place) in enumerate(zip(gradients, places)):
        here = rows((*place, True))

        def weight(piece, index=index, here=here):
            at = sum(SPLIT[:piece])
            own = rows_of(weights[piece], here.start, block)
            other = lambda lane: theirs[index * block : (index + 1) * block, at + lane : at + lane + LANES]
            if index + 1 < len(places):
                return other
            return lambda lane: own(lane) + other(lane)

        full[here, :] += dots(gradient, [weight(piece) for piece in range(len(weights))])
    out[...] = jnp.sum(full[...].T, axis=0, keepdims=True)


def in_vmem(array):
    return pltpu.with_memory_space_constraint(array, pltpu.VMEM)


def body(units, query_grad, out_grads, inputs):
    ahead, across, twin = pairs_of(units)
    send = lambda value, pairs: lax.ppermute(value, "unit", pairs)
    block, outputs = out_grads.shape
    tokens = inputs.shape[0]

    weights = []
    q = pltpu.with_memory_space_constraint(query_grad, pltpu.HBM)
    state = [pltpu.with_memory_space_constraint(inputs, pltpu.HBM), None]

    def piece(*after):
        if len(weights) == len(SPLIT):
            return
        made = list(weigh(len(weights), state[0], q, state[1], after))
        if not weights:
            state[0] = in_vmem(made.pop(0))
        weights.append(in_vmem(made.pop(0)))
        state[1] = in_vmem(made[0]) if made else None

    def later(value):
        return lax.optimization_barrier((value, weights[-1]))[0]

    hops = units // 4
    held, places = [out_grads], [(0, True)]
    same, other = send(out_grads, ahead), send(out_grads, across)
    piece()
    for hop in range(1, hops):
        held += [same, other]
        places += [(hop, True), (hop, False)]
        if hop + 1 == hops:
            last = send(later(same), ahead)
            break
        next_same = send(later(same), ahead)
        if hop > 1:
            piece(same)
        next_other = send(later(other) if hop > 1 else other, ahead)
        if hop == 1:
            piece(same, other)
        else:
            piece(other)
        same, other = next_same, next_other

    ends = places[-1:] + [(hops, True)]
    theirs = pl.pallas_call(
        functools.partial(give_kernel, units, ends),
        in_specs=[VMEM] * len(weights),
        out_specs=VMEM,
        out_shape=jax.ShapeDtypeStruct((len(ends) * block, outputs), jnp.float32),
        compiler_params=pltpu.CompilerParams(vmem_limit_bytes=GRANT),
    )(*weights)
    theirs = send(theirs, twin)
    given = send(stack([lax.optimization_barrier((out_grads, weights[2]))[0]] + held[1:-2]), twin)
    more = send(held[-2], twin)

    mine = [((*place, True), array, 0) for place, array in zip(places, held)]
    others = [((*place, False), given, index * block) for index, place in enumerate(places[:-2])]
    others.append(((*places[-2], False), more, 0))
    table = None
    for found, flops in ((mine, TABLE_FLOPS), (others, 0)):
        for group in range(0, len(found), GROUP):
            table = add_blocks(units, block, found[group : group + GROUP], weights, table, flops)
    partial_value = pl.pallas_call(
        functools.partial(last_kernel, units, block, ends),
        in_specs=[VMEM] * (4 + len(weights)),
        out_specs=VMEM,
        out_shape=jax.ShapeDtypeStruct((1, tokens), jnp.float32),
        scratch_shapes=[pltpu.VMEM((tokens, LANES), jnp.float32)],
        compiler_params=pltpu.CompilerParams(vmem_limit_bytes=GRANT),
    )(held[-1], last, theirs, table, *weights)

    bit = 1
    while bit < units:
        pairs = [(unit, unit ^ bit) for unit in range(units)]
        partial_value += send(partial_value, pairs)
        bit *= 2
    return partial_value.reshape(tokens)


def solution(mesh):
    return jax.shard_map(
        functools.partial(body, mesh.shape["unit"]),
        mesh=mesh,
        in_specs=(P("job", "unit"), P(("job", "unit"), None), P("job", "unit")),
        out_specs=P("job"),
        check_vma=False,
    )
```

```python
import functools

import jax
import jax.numpy as jnp
from jax import lax
from jax.experimental import pallas as pl
from jax.experimental.pallas import tpu as pltpu
from jax.sharding import PartitionSpec as P

SPLIT = (1024, 3072, 2560, 1536)
FETCH = 512
STEP = 1280
LANES = 128
GROUP = 16
HIDDEN_FLOPS = 2 * 10**10
GRANT = 8 << 20
VMEM = pl.BlockSpec(memory_space=pltpu.VMEM)
HBM = pl.BlockSpec(memory_space=pltpu.HBM)
ANY = pl.BlockSpec(memory_space=pl.ANY)


def place_of(units, unit):
    chips = units // 2
    chip = unit // 2
    if units != 16:
        return chip
    odd = chip % 2
    return (1 - odd) * (chip // 2) + odd * (chips - 1 - chip // 2)


def unit_at(units, place, core):
    chips = units // 2
    place = lax.rem(place + 2 * chips, chips)
    if units != 16:
        return 2 * place + core
    back = place // (chips // 2)
    return 2 * ((1 - back) * 2 * place + back * (2 * (chips - 1 - place) + 1)) + core


def block_of(units, hop, same, mine):
    unit = lax.axis_index("unit")
    core = lax.rem(unit, 2)
    holder = core if mine else 1 - core
    place = place_of(units, unit)
    if hop == 0:
        return unit_at(units, place, holder)
    behind = 1 - lax.rem(holder + hop, 2)
    return unit_at(units, place + (1 - 2 * behind) * hop, 1 - behind if same else behind)


def pairs_of(units):
    chips = units // 2
    walk = sorted(range(chips), key=lambda chip: place_of(units, 2 * chip))
    at = lambda place, core: 2 * walk[place % chips] + core
    ahead, beside, twin = ([], []), [], []
    for place in range(chips):
        for core, way in ((0, 1), (1, -1)):
            ahead[1].append((at(place, core), at(place + way, 1 - core)))
            ahead[0].append((at(place, core), at(place - way, 1 - core)))
            beside.append((at(place, 1 - core), at(place + way, 1 - core)))
            twin.append((at(place, core), at(place, 1 - core)))
    return ahead, beside, twin


def product(rows, columns):
    return lax.dot_general(rows, columns, (((1,), (1,)), ((), ())), preferred_element_type=jnp.float32)


def fetches(q_ref, first, count, to, sems):
    return [
        pltpu.make_async_copy(
            q_ref.at[pl.ds(first + at, FETCH)], to.at[pl.ds(at, FETCH)], sems.at[at // FETCH]
        )
        for at in range(0, count, FETCH)
    ]


def first_kernel(width, following, x_ref, q_ref, x, weights, slab, own, placed, ready, coming):
    move = pltpu.make_async_copy(x_ref, x, placed)
    move.start()
    mine = fetches(q_ref, 0, width, own, ready)
    later = fetches(q_ref, width, following, slab, coming)
    for copy in mine + later:
        copy.start()
    move.wait()
    for index, copy in enumerate(mine):
        copy.wait()
        at = slice(index * FETCH, (index + 1) * FETCH)
        weights[:, at] = product(x[...], own[at, :])
    for copy in later:
        copy.wait()


def next_kernel(first, width, following, waits, x, q_ref, slab, *refs):
    weights = refs[waits]
    later = []
    if following:
        later = fetches(q_ref, first + width, following, refs[waits + 1], refs[-1])
    for copy in later:
        copy.start()

    step = max(step for step in range(LANES, STEP + 1, LANES) if width % step == 0)

    @pl.loop(0, width // step)
    def _(i):
        at = pl.ds(pl.multiple_of(i * step, step), step)
        weights[:, at] = product(x[...], slab[at, :])

    for copy in later:
        copy.wait()


def weigh(piece, x, q, slab, after):
    tokens, depth = x.shape
    first, width = sum(SPLIT[:piece]), SPLIT[piece]
    following = SPLIT[piece + 1] if piece + 1 < len(SPLIT) else 0
    out_shape = [pltpu.VMEM((tokens, width), jnp.float32)]
    scratch = []
    if following:
        out_shape.append(pltpu.VMEM((following, depth), q.dtype))
        scratch = [pltpu.SemaphoreType.DMA((following // FETCH,))]
    if piece:
        kernel = functools.partial(next_kernel, first, width, following, len(after))
        operands = [x, q, slab, *after]
        in_specs = [VMEM, HBM, VMEM] + [ANY] * len(after)
    else:
        kernel = functools.partial(first_kernel, width, following)
        operands = [x, q]
        in_specs = [HBM, HBM]
        out_shape.insert(0, pltpu.VMEM(x.shape, x.dtype))
        scratch = [
            pltpu.VMEM((width, depth), q.dtype),
            pltpu.SemaphoreType.DMA,
            pltpu.SemaphoreType.DMA((width // FETCH,)),
        ] + scratch
    return pl.pallas_call(
        kernel,
        in_specs=in_specs,
        out_specs=[VMEM] * len(out_shape),
        out_shape=out_shape,
        scratch_shapes=scratch,
        compiler_params=pltpu.CompilerParams(vmem_limit_bytes=GRANT),
        cost_estimate=pl.CostEstimate(
            flops=2 * tokens * depth * width,
            bytes_accessed=2 * depth * width,
            transcendentals=0,
        ),
    )(*operands)


def dots(gradient, weights):
    total = jnp.zeros((gradient.shape[0], LANES), jnp.float32)
    at = 0
    for width, weight in zip(SPLIT, weights):
        for lane in range(0, width, LANES):
            total += gradient[:, at : at + LANES].astype(jnp.float32) * weight(lane)
            at += LANES
    return total


def rows_of(ref, start, block):
    return lambda lane: ref[pl.ds(start, block), lane : lane + LANES]


def stack_kernel(*refs):
    out, at = refs[-1], 0
    for ref in refs[:-1]:
        out[at : at + ref.shape[0], :] = ref[...]
        at += ref.shape[0]


def stack(arrays):
    rows = sum(array.shape[0] for array in arrays)
    return pl.pallas_call(
        stack_kernel,
        in_specs=[VMEM] * len(arrays),
        out_specs=VMEM,
        out_shape=jax.ShapeDtypeStruct((rows, arrays[0].shape[1]), arrays[0].dtype),
        compiler_params=pltpu.CompilerParams(vmem_limit_bytes=GRANT),
    )(*arrays)


def table_kernel(units, block, places, fresh, *refs):
    count = 1 + max(array for array, _, _ in places)
    gradients, weights, table = refs[:count], refs[count : count + len(SPLIT)], refs[-1]
    table[...] = jnp.zeros_like(table) if fresh else refs[-2][...]
    for array, row, place in places:
        start = pl.multiple_of(block_of(units, *place) * block, block)
        gradient = gradients[array][row : row + block, :]
        table[pl.ds(start, block), :] = dots(gradient, [rows_of(ref, start, block) for ref in weights])


def add_blocks(units, block, found, weights, table):
    shape = (weights[0].shape[0], LANES)
    arrays, places = [], []
    for place, array, row in found:
        if not any(array is known for known in arrays):
            arrays.append(array)
        index = [array is known for known in arrays].index(True)
        places.append((index, row, place))
    extra = [] if table is None else [table]
    return pl.pallas_call(
        functools.partial(table_kernel, units, block, places, table is None),
        in_specs=[VMEM] * (len(arrays) + len(weights) + len(extra)),
        out_specs=VMEM,
        out_shape=jax.ShapeDtypeStruct(shape, jnp.float32),
        compiler_params=pltpu.CompilerParams(vmem_limit_bytes=GRANT),
        cost_estimate=pl.CostEstimate(flops=0, bytes_accessed=0, transcendentals=0),
    )(*arrays, *weights, *extra)


def give_kernel(units, places, *refs):
    weights, out = refs[:-1], refs[-1]
    block = out.shape[0] // len(places)
    for index, place in enumerate(places):
        start = pl.multiple_of(block_of(units, *place, False) * block, block)
        at = 0
        for ref in weights:
            out[index * block : (index + 1) * block, at : at + ref.shape[1]] = ref[pl.ds(start, block), :]
            at += ref.shape[1]


def arrival_kernel(last, table, out):
    out[...] = jnp.zeros_like(out)


def last_kernel(units, block, places, mores, arrived, *refs):
    gradients, refs = refs[: len(places)], refs[len(places) :]
    given, more, theirs, table, *weights, out, full = refs
    full[...] = table[...]

    def rows(place):
        return pl.ds(pl.multiple_of(block_of(units, *place) * block, block), block)

    for index, place in enumerate(mores):
        here = rows((*place, False))
        late = index + 1 == len(mores)
        gradient = more[...] if late else given[index * block : (index + 1) * block, :]
        full[here, :] = dots(gradient, [rows_of(ref, here.start, block) for ref in weights])
    for index, (gradient, place) in enumerate(zip(gradients, places)):
        here = rows((*place, True))

        def weight(piece, index=index, here=here):
            at = sum(SPLIT[:piece])
            own = rows_of(weights[piece], here.start, block)
            other = lambda lane: theirs[index * block : (index + 1) * block, at + lane : at + lane + LANES]
            if index + 1 < len(places):
                return other
            return lambda lane: own(lane) + other(lane)

        full[here, :] += dots(gradient, [weight(piece) for piece in range(len(weights))])
    out[...] = jnp.sum(full[...].T, axis=0, keepdims=True)


def in_vmem(array):
    return pltpu.with_memory_space_constraint(array, pltpu.VMEM)


def body(units, query_grad, out_grads, inputs):
    ahead, beside, twin = pairs_of(units)
    send = lambda value, pairs: lax.ppermute(value, "unit", pairs)
    block, outputs = out_grads.shape
    tokens = inputs.shape[0]

    weights = []
    q = pltpu.with_memory_space_constraint(query_grad, pltpu.HBM)
    state = [pltpu.with_memory_space_constraint(inputs, pltpu.HBM), None]

    def piece(*after):
        if len(weights) == len(SPLIT):
            return
        made = list(weigh(len(weights), state[0], q, state[1], after))
        if not weights:
            state[0] = in_vmem(made.pop(0))
        weights.append(in_vmem(made.pop(0)))
        state[1] = in_vmem(made[0]) if made else None

    def later(value):
        return lax.optimization_barrier((value, weights[-1]))[0]

    hops = units // 4
    held, places = [out_grads], [(0, True)]
    same, other = send(out_grads, ahead[1]), send(out_grads, beside)
    piece()
    for hop in range(1, hops):
        held += [same, other]
        places += [(hop, True), (hop, False)]
        if hop + 1 == hops:
            last = send(same, ahead[hops % 2])
            piece(same)
            break
        next_same = send(later(same), ahead[(hop + 1) % 2])
        if hop > 1:
            piece(same)
        next_other = send(later(other) if hop > 1 else other, ahead[(hop + 1) % 2])
        if hop == 1:
            piece(same, other)
        same, other = next_same, next_other

    ends = places[-1:] + [(hops, True)]
    theirs = pl.pallas_call(
        functools.partial(give_kernel, units, ends),
        in_specs=[VMEM] * len(weights),
        out_specs=VMEM,
        out_shape=jax.ShapeDtypeStruct((len(ends) * block, outputs), jnp.float32),
        compiler_params=pltpu.CompilerParams(vmem_limit_bytes=GRANT),
    )(*weights)
    theirs = send(theirs, twin)
    given = send(stack([lax.optimization_barrier((out_grads, weights[2]))[0]] + held[1:-2]), twin)
    more = send(held[-2], twin)

    found = [((*place, True), array, 0) for place, array in zip(places, held)]
    table = None
    for group in range(0, len(found), GROUP):
        table = add_blocks(units, block, found[group : group + GROUP], weights, table)
    arrived = pl.pallas_call(
        arrival_kernel,
        in_specs=[ANY, ANY],
        out_specs=VMEM,
        out_shape=jax.ShapeDtypeStruct((8, LANES), jnp.float32),
        compiler_params=pltpu.CompilerParams(vmem_limit_bytes=GRANT),
        cost_estimate=pl.CostEstimate(flops=HIDDEN_FLOPS, bytes_accessed=0, transcendentals=0),
    )(last, table)
    partial_value = pl.pallas_call(
        functools.partial(last_kernel, units, block, ends, places[:-1]),
        in_specs=[ANY] + [VMEM] * (6 + len(weights)),
        out_specs=VMEM,
        out_shape=jax.ShapeDtypeStruct((1, tokens), jnp.float32),
        scratch_shapes=[pltpu.VMEM((tokens, LANES), jnp.float32)],
        compiler_params=pltpu.CompilerParams(vmem_limit_bytes=GRANT),
    )(arrived, held[-1], last, given, more, theirs, table, *weights)

    bit = 1
    while bit < units:
        pairs = [(unit, unit ^ bit ^ (bit > 1)) for unit in range(units)]
        partial_value += send(partial_value, pairs)
        bit *= 2
    return partial_value.reshape(tokens)


def solution(mesh):
    return jax.shard_map(
        functools.partial(body, mesh.shape["unit"]),
        mesh=mesh,
        in_specs=(P("job", "unit"), P(("job", "unit"), None), P("job", "unit")),
        out_specs=P("job"),
        check_vma=False,
    )
```

```python
import functools

import jax
import jax.numpy as jnp
from jax import lax
from jax.experimental import pallas as pl
from jax.experimental.pallas import tpu as pltpu
from jax.sharding import PartitionSpec as P

SPLIT = (1024, 3072, 2560, 1536)
FETCH = 512
STEP = 1280
LANES = 128
GROUP = 16
HIDDEN_FLOPS = 2 * 10**10
GRANT = 8 << 20
VMEM = pl.BlockSpec(memory_space=pltpu.VMEM)
HBM = pl.BlockSpec(memory_space=pltpu.HBM)
ANY = pl.BlockSpec(memory_space=pl.ANY)


def place_of(units, unit):
    chips = units // 2
    chip = unit // 2
    if units != 16:
        return chip
    odd = chip % 2
    return (1 - odd) * (chip // 2) + odd * (chips - 1 - chip // 2)


def unit_at(units, place, core):
    chips = units // 2
    place = lax.rem(place + 2 * chips, chips)
    if units != 16:
        return 2 * place + core
    back = place // (chips // 2)
    return 2 * ((1 - back) * 2 * place + back * (2 * (chips - 1 - place) + 1)) + core


def block_of(units, hop, same, mine):
    unit = lax.axis_index("unit")
    core = lax.rem(unit, 2)
    holder = core if mine else 1 - core
    place = place_of(units, unit)
    if hop == 0:
        return unit_at(units, place, holder)
    behind = 1 - lax.rem(holder + hop, 2)
    return unit_at(units, place + (1 - 2 * behind) * hop, 1 - behind if same else behind)


def pairs_of(units):
    chips = units // 2
    walk = sorted(range(chips), key=lambda chip: place_of(units, 2 * chip))
    at = lambda place, core: 2 * walk[place % chips] + core
    ahead, beside, twin = ([], []), [], []
    for place in range(chips):
        for core, way in ((0, 1), (1, -1)):
            ahead[1].append((at(place, core), at(place + way, 1 - core)))
            ahead[0].append((at(place, core), at(place - way, 1 - core)))
            beside.append((at(place, 1 - core), at(place + way, 1 - core)))
            twin.append((at(place, core), at(place, 1 - core)))
    return ahead, beside, twin


def product(rows, columns):
    return lax.dot_general(rows, columns, (((1,), (1,)), ((), ())), preferred_element_type=jnp.float32)


def fetches(q_ref, first, count, to, sems):
    return [
        pltpu.make_async_copy(
            q_ref.at[pl.ds(first + at, FETCH)], to.at[pl.ds(at, FETCH)], sems.at[at // FETCH]
        )
        for at in range(0, count, FETCH)
    ]


def first_kernel(width, following, x_ref, q_ref, x, weights, slab, own, placed, ready, coming):
    move = pltpu.make_async_copy(x_ref, x, placed)
    move.start()
    mine = fetches(q_ref, 0, width, own, ready)
    later = fetches(q_ref, width, following, slab, coming)
    for copy in mine + later:
        copy.start()
    move.wait()
    for index, copy in enumerate(mine):
        copy.wait()
        at = slice(index * FETCH, (index + 1) * FETCH)
        weights[:, at] = product(x[...], own[at, :])
    for copy in later:
        copy.wait()


def next_kernel(first, width, following, waits, x, q_ref, slab, *refs):
    weights = refs[waits]
    later = []
    if following:
        later = fetches(q_ref, first + width, following, refs[waits + 1], refs[-1])
    for copy in later:
        copy.start()

    step = max(step for step in range(LANES, STEP + 1, LANES) if width % step == 0)

    @pl.loop(0, width // step)
    def _(i):
        at = pl.ds(pl.multiple_of(i * step, step), step)
        weights[:, at] = product(x[...], slab[at, :])

    for copy in later:
        copy.wait()


def weigh(piece, x, q, slab, after):
    tokens, depth = x.shape
    first, width = sum(SPLIT[:piece]), SPLIT[piece]
    following = SPLIT[piece + 1] if piece + 1 < len(SPLIT) else 0
    out_shape = [pltpu.VMEM((tokens, width), jnp.float32)]
    scratch = []
    if following:
        out_shape.append(pltpu.VMEM((following, depth), q.dtype))
        scratch = [pltpu.SemaphoreType.DMA((following // FETCH,))]
    if piece:
        kernel = functools.partial(next_kernel, first, width, following, len(after))
        operands = [x, q, slab, *after]
        in_specs = [VMEM, HBM, VMEM] + [ANY] * len(after)
    else:
        kernel = functools.partial(first_kernel, width, following)
        operands = [x, q]
        in_specs = [HBM, HBM]
        out_shape.insert(0, pltpu.VMEM(x.shape, x.dtype))
        scratch = [
            pltpu.VMEM((width, depth), q.dtype),
            pltpu.SemaphoreType.DMA,
            pltpu.SemaphoreType.DMA((width // FETCH,)),
        ] + scratch
    return pl.pallas_call(
        kernel,
        in_specs=in_specs,
        out_specs=[VMEM] * len(out_shape),
        out_shape=out_shape,
        scratch_shapes=scratch,
        compiler_params=pltpu.CompilerParams(vmem_limit_bytes=GRANT),
        cost_estimate=pl.CostEstimate(
            flops=2 * tokens * depth * width,
            bytes_accessed=2 * depth * width,
            transcendentals=0,
        ),
    )(*operands)


def dots(gradient, weights):
    total = jnp.zeros((gradient.shape[0], LANES), jnp.float32)
    at = 0
    for width, weight in zip(SPLIT, weights):
        for lane in range(0, width, LANES):
            total += gradient[:, at : at + LANES].astype(jnp.float32) * weight(lane)
            at += LANES
    return total


def rows_of(ref, start, block):
    return lambda lane: ref[pl.ds(start, block), lane : lane + LANES]


def stack_kernel(*refs):
    out, at = refs[-1], 0
    for ref in refs[:-1]:
        out[at : at + ref.shape[0], :] = ref[...]
        at += ref.shape[0]


def stack(arrays):
    rows = sum(array.shape[0] for array in arrays)
    return pl.pallas_call(
        stack_kernel,
        in_specs=[VMEM] * len(arrays),
        out_specs=VMEM,
        out_shape=jax.ShapeDtypeStruct((rows, arrays[0].shape[1]), arrays[0].dtype),
        compiler_params=pltpu.CompilerParams(vmem_limit_bytes=GRANT),
    )(*arrays)


def table_kernel(units, block, places, fresh, *refs):
    count = 1 + max(array for array, _, _ in places)
    gradients, weights, table = refs[:count], refs[count : count + len(SPLIT)], refs[-1]
    table[...] = jnp.zeros_like(table) if fresh else refs[-2][...]
    for array, row, place in places:
        start = pl.multiple_of(block_of(units, *place) * block, block)
        gradient = gradients[array][row : row + block, :]
        table[pl.ds(start, block), :] = dots(gradient, [rows_of(ref, start, block) for ref in weights])


def add_blocks(units, block, found, weights, table):
    shape = (weights[0].shape[0], LANES)
    arrays, places = [], []
    for place, array, row in found:
        if not any(array is known for known in arrays):
            arrays.append(array)
        index = [array is known for known in arrays].index(True)
        places.append((index, row, place))
    extra = [] if table is None else [table]
    return pl.pallas_call(
        functools.partial(table_kernel, units, block, places, table is None),
        in_specs=[VMEM] * (len(arrays) + len(weights) + len(extra)),
        out_specs=VMEM,
        out_shape=jax.ShapeDtypeStruct(shape, jnp.float32),
        compiler_params=pltpu.CompilerParams(vmem_limit_bytes=GRANT),
        cost_estimate=pl.CostEstimate(flops=0, bytes_accessed=0, transcendentals=0),
    )(*arrays, *weights, *extra)


def give_kernel(units, places, *refs):
    weights, out = refs[:-1], refs[-1]
    block = out.shape[0] // len(places)
    for index, place in enumerate(places):
        start = pl.multiple_of(block_of(units, *place, False) * block, block)
        at = 0
        for ref in weights:
            out[index * block : (index + 1) * block, at : at + ref.shape[1]] = ref[pl.ds(start, block), :]
            at += ref.shape[1]


def arrival_kernel(last, table, out):
    out[...] = jnp.zeros_like(out)


def last_kernel(units, block, places, mores, arrived, *refs):
    gradients, refs = refs[: len(places)], refs[len(places) :]
    given, more, theirs, table, *weights, out, full = refs
    full[...] = table[...]

    def rows(place):
        return pl.ds(pl.multiple_of(block_of(units, *place) * block, block), block)

    for index, place in enumerate(mores):
        here = rows((*place, False))
        late = index + 1 == len(mores)
        gradient = more[...] if late else given[index * block : (index + 1) * block, :]
        full[here, :] = dots(gradient, [rows_of(ref, here.start, block) for ref in weights])
    for index, (gradient, place) in enumerate(zip(gradients, places)):
        here = rows((*place, True))

        def weight(piece, index=index, here=here):
            at = sum(SPLIT[:piece])
            own = rows_of(weights[piece], here.start, block)
            other = lambda lane: theirs[index * block : (index + 1) * block, at + lane : at + lane + LANES]
            if index + 1 < len(places):
                return other
            return lambda lane: own(lane) + other(lane)

        full[here, :] += dots(gradient, [weight(piece) for piece in range(len(weights))])
    out[...] = jnp.sum(full[...].T, axis=0, keepdims=True)


def in_vmem(array):
    return pltpu.with_memory_space_constraint(array, pltpu.VMEM)


def body(units, query_grad, out_grads, inputs):
    ahead, beside, twin = pairs_of(units)
    send = lambda value, pairs: lax.ppermute(value, "unit", pairs)
    block, outputs = out_grads.shape
    tokens = inputs.shape[0]

    weights = []
    q = pltpu.with_memory_space_constraint(query_grad, pltpu.HBM)
    state = [pltpu.with_memory_space_constraint(inputs, pltpu.HBM), None]

    def piece(*after):
        if len(weights) == len(SPLIT):
            return
        made = list(weigh(len(weights), state[0], q, state[1], after))
        if not weights:
            state[0] = in_vmem(made.pop(0))
        weights.append(in_vmem(made.pop(0)))
        state[1] = in_vmem(made[0]) if made else None

    def later(value):
        return lax.optimization_barrier((value, weights[-1]))[0]

    hops = units // 4
    held, places = [out_grads], [(0, True)]
    same, other = send(out_grads, ahead[1]), send(out_grads, beside)
    piece()
    for hop in range(1, hops):
        held += [same, other]
        places += [(hop, True), (hop, False)]
        if hop + 1 == hops:
            last = send(same, ahead[hops % 2])
            piece(same)
            break
        next_same = send(later(same), ahead[(hop + 1) % 2])
        if hop > 1:
            piece(same)
        next_other = send(later(other) if hop > 1 else other, ahead[(hop + 1) % 2])
        if hop == 1:
            piece(same, other)
        same, other = next_same, next_other

    ends = places[-1:] + [(hops, True)]
    theirs = pl.pallas_call(
        functools.partial(give_kernel, units, ends),
        in_specs=[VMEM] * len(weights),
        out_specs=VMEM,
        out_shape=jax.ShapeDtypeStruct((len(ends) * block, outputs), jnp.float32),
        compiler_params=pltpu.CompilerParams(vmem_limit_bytes=GRANT),
    )(*weights)
    theirs = send(theirs, twin)
    given = send(stack([lax.optimization_barrier((out_grads, weights[2]))[0]] + held[1:-2]), twin)
    more = send(held[-2], twin)

    found = [((*place, True), array, 0) for place, array in zip(places, held)]
    table = None
    for group in range(0, len(found), GROUP):
        table = add_blocks(units, block, found[group : group + GROUP], weights, table)
    arrived = pl.pallas_call(
        arrival_kernel,
        in_specs=[ANY, ANY],
        out_specs=VMEM,
        out_shape=jax.ShapeDtypeStruct((8, LANES), jnp.float32),
        compiler_params=pltpu.CompilerParams(vmem_limit_bytes=GRANT),
        cost_estimate=pl.CostEstimate(flops=HIDDEN_FLOPS, bytes_accessed=0, transcendentals=0),
    )(last, table)
    partial_value = pl.pallas_call(
        functools.partial(last_kernel, units, block, ends, places[:-1]),
        in_specs=[ANY] + [VMEM] * (6 + len(weights)),
        out_specs=VMEM,
        out_shape=jax.ShapeDtypeStruct((1, tokens), jnp.float32),
        scratch_shapes=[pltpu.VMEM((tokens, LANES), jnp.float32)],
        compiler_params=pltpu.CompilerParams(vmem_limit_bytes=GRANT),
    )(arrived, held[-1], last, given, more, theirs, table, *weights)

    def moved(bits):
        return send(partial_value, [(unit, unit ^ bits) for unit in range(units)])

    partial_value += moved(1)
    far, both, near = moved(5), moved(7), moved(3)
    partial_value = (partial_value + far) + (both + near)
    bit = 8
    while bit < units:
        partial_value += moved(bit + 1)
        bit *= 2
    return partial_value.reshape(tokens)


def solution(mesh):
    return jax.shard_map(
        functools.partial(body, mesh.shape["unit"]),
        mesh=mesh,
        in_specs=(P("job", "unit"), P(("job", "unit"), None), P("job", "unit")),
        out_specs=P("job"),
        check_vma=False,
    )
```
